128 devices in a mesh: ctx: 8 (over y, core), batch: 16 (over x, z).
Axes of the slice: x: 4, y: 4, z: 4, core: 2. Of those that a mesh axis runs over, the one named last changes fastest.
Arguments:
- queries: bfloat16 [512, 8192], P('batch'), may hold values from -200 to 200
- seq_doc: int32 [512, 1], P('batch'), may hold values from 0 to 3; in each aligned block of 32 rows (0 to 31, 32 to 63, ...) at most 16 rows name the same one
- suffix_lengths: int32 [512], P('batch'), may hold values from 1 to 32, as said below
- prefix_keys: bfloat16 [16, 8192, 1024], P('batch', 'ctx'), may hold values from -6 to 6
- prefix_values: bfloat16 [16, 8192, 1024], P('batch', 'ctx'), may hold values from -6 to 6
- suffix_keys: bfloat16 [512, 32, 1024], P('batch'), may hold values from -9 to 9
- suffix_values: bfloat16 [512, 32, 1024], P('batch'), may hold values from -6 to 6
Outputs:
- attended: bfloat16 [512, 8192], P('batch')
The draws below stay inside these ranges and needn't reach their ends.
Inputs may be any that keep to these rules, and one draw needn't show every extreme that they name: `seq_doc`: among the rows of one index of batch, no document is read by more than 16 sequences. Sequence r's private suffix holds the first suffix_lengths[r] positions of its cache.
All inputs are finite; a program needn't handle non-finite values.
Results may differ from the reference program's by a relative error of at most 0.014.
Values may be sent and summed in bfloat16 or wider, within the bound.
A program may use at most 192 MiB of HBM per device.

```python
import math
import jax
import jax.numpy as jnp
import numpy as np
from jax import lax

H = 64
KVH = 8
HD = 128
DOCS = 4
SEQ_DEV = 32
SLEN = 32
MOST = 16
SEQS = 512
GROUP = 4
BLEN = 8192
PLEN = 32768
N_BATCH = 16


def prefix_base(key):
    return jnp.clip(jax.random.normal(key, (DOCS, PLEN, KVH * HD), jnp.float32), -6.0, 6.0)


def draw_prefix_keys(key, part):
    base_keys = prefix_base(key)
    return base_keys.reshape(DOCS * GROUP, BLEN, KVH * HD).astype(jnp.bfloat16)


def draw_queries(key, part):
    key = jax.random.fold_in(key, 2)
    noise_key = jax.random.fold_in(key, 0)
    drawn_values = jnp.clip(2.5 * jax.random.normal(noise_key, (SEQS, H * HD), jnp.float32), -15.0, 15.0)
    return drawn_values.astype(jnp.bfloat16)


def draw_suffix_lengths(key, part):
    key = jax.random.fold_in(key, 5)
    length_key, row_key = jax.random.split(key)
    drawn_lengths = jax.random.randint(length_key, (SEQS,), 1, SLEN + 1)
    full_row = jax.random.randint(row_key, (), 0, SEQS)
    drawn_lengths = jnp.where(jnp.arange(SEQS) == full_row, SLEN, drawn_lengths)
    return drawn_lengths.astype(jnp.int32)


def shard_levels(own_key, extent, cuts, low, top_value):
    gain, own = 1.0, jax.random.fold_in(own_key, 6)
    for position, blocks in cuts:
        steps = jnp.exp(jax.random.uniform(jax.random.fold_in(own, position), (blocks,), jnp.float32, low / len(cuts), top_value / len(cuts)))
        gain = gain * jnp.repeat(steps, extent[position] // blocks).reshape([-1 if axis == position else 1 for axis in range(len(extent))])
    return gain


def deal_out(own_key, own, number, rows, count, top, limit, skew):
    order = jax.random.permutation(own_key, count)
    heavy_load, ordinary = load_shares(count, rows * top, limit, skew, True), load_shares(count, rows * top, limit, skew, False)
    places = jnp.arange(count)

    def named(lengths, rotation):
        used = int((lengths > 0).sum())
        fixed = max(1, used // 4)
        moved = fixed + (places - fixed + rotation * (used - fixed)) % max(1, count - fixed)
        return jnp.zeros((count,), jnp.int32).at[order[jnp.where(places < fixed, places, moved)]].set(jnp.asarray(lengths, jnp.int32))

    lengths = jnp.where(number % 4 == 0, named(heavy_load, number // 4), named(ordinary, number - number // 4 - 1))
    mixed = jax.random.permutation(jax.random.fold_in(own, 3), count)
    donor, sink = mixed[0:count // 2 * 2:2], mixed[1:count // 2 * 2:2]
    slack = jnp.minimum(lengths[donor] - 1, limit - lengths[sink]) // 2
    slack = jnp.where((donor == order[0]) | (sink == order[0]) | (lengths[sink] == 0), 0, jnp.maximum(slack, 0))
    moved = jax.random.randint(jax.random.fold_in(own, 4), (count // 2,), 0, 1 << 20) % (slack + 1)
    lengths = lengths.at[donor].add(-moved).at[sink].add(moved)
    labels = jnp.searchsorted(jnp.cumsum(lengths), jnp.arange(rows * top), side="right").astype(jnp.int32)
    table = labels.reshape(top, rows).T
    table = table[jax.random.permutation(jax.random.fold_in(own, 1), rows)]
    rotation = jax.random.randint(jax.random.fold_in(own, 2), (rows, 1), 0, top)
    return jnp.take_along_axis(table, (jnp.arange(top)[None, :] + rotation) % top, axis=1)


def load_shares(number_of, total, reach, skew, full):
    loads = [(1 << 20) // math.isqrt(grade ** skew) + 1 for grade in range(1, number_of + 1)]
    largest = reach if full else min(reach, max(-(-total // number_of), total * loads[0] // sum(loads)))
    least = 1 if total - largest >= number_of - 1 else 0
    holding, spare = [largest] + [least] * (number_of - 1), total - largest - least * (number_of - 1)
    while spare > 0:
        movable = [i for i in range(1, number_of) if holding[i] < largest] or [i for i in range(1, number_of) if holding[i] < reach]
        mass, budget = sum([loads[i] for i in movable]), spare
        for i in movable:
            more = min(reach - holding[i], max(1, budget * loads[i] // mass), spare)
            holding[i] = holding[i] + more
            spare = spare - more
    return np.array(holding)


def normal_values(key, dims, deviation, bound, shards=(), kind=jnp.bfloat16):
    values = jax.random.normal(key, dims, jnp.float32) * deviation
    if len(shards) > 0:
        values = shard_levels(key, dims, shards, -0.22, 0.18) * values
    return jnp.clip(values, min=-bound, max=bound).astype(kind)


def setup_inputs(seed: int = 0) -> dict:
    streams_of = jax.random.split(jax.random.key(seed), 8)
    queries = draw_queries(jax.random.fold_in(streams_of[7], 71), 0)
    seq_doc_keys = jax.random.split(jax.random.fold_in(streams_of[1], 1), SEQS // SEQ_DEV)
    seq_doc_turns = jax.random.permutation(jax.random.fold_in(streams_of[1], 3), SEQS // SEQ_DEV)
    seq_doc = jax.vmap(lambda own, number: deal_out(jax.random.fold_in(streams_of[1], 2), own, number, SEQ_DEV, DOCS, 1, MOST, 2))(seq_doc_keys, seq_doc_turns).reshape((SEQS, 1))
    suffix_lengths = draw_suffix_lengths(jax.random.fold_in(streams_of[7], 71), 0)
    prefix_keys = draw_prefix_keys(jax.random.fold_in(streams_of[7], 71), 0)
    prefix_values = normal_values(streams_of[4], (N_BATCH, BLEN, KVH * HD), 1.0, 6.0, ((0, 16), (1, 8)))
    suffix_keys = normal_values(streams_of[5], (SEQS, SLEN, KVH * HD), 1.5, 9.0, ((0, 16),))
    suffix_values = normal_values(streams_of[6], (SEQS, SLEN, KVH * HD), 1.0, 6.0, ((0, 16),))
    return {"queries": queries, "seq_doc": seq_doc, "suffix_lengths": suffix_lengths, "prefix_keys": prefix_keys, "prefix_values": prefix_values, "suffix_keys": suffix_keys, "suffix_values": suffix_values}


def reference(queries, seq_doc, suffix_lengths, prefix_keys, prefix_values, suffix_keys, suffix_values):
    score_scale = HD ** -0.5

    def one_row(inputs):
        query_row, doc_id, length, row_keys, row_values = inputs
        query_heads = query_row.astype(jnp.float32).reshape(KVH, H // KVH, HD)
        first_block = (doc_id * GROUP).astype(jnp.int32)
        doc_keys = lax.dynamic_slice_in_dim(prefix_keys, first_block, GROUP, 0).astype(jnp.float32).reshape(PLEN, KVH, HD)
        doc_values = lax.dynamic_slice_in_dim(prefix_values, first_block, GROUP, 0).astype(jnp.float32).reshape(PLEN, KVH, HD)
        cache_keys = row_keys.astype(jnp.float32).reshape(SLEN, KVH, HD)
        cache_values = row_values.astype(jnp.float32).reshape(SLEN, KVH, HD)
        prefix_scores = jnp.einsum("kgd,pkd->kgp", query_heads, doc_keys) * score_scale
        suffix_scores = jnp.einsum("kgd,tkd->kgt", query_heads, cache_keys) * score_scale
        in_cache = jnp.arange(SLEN, dtype=jnp.int32) < length
        suffix_scores = jnp.where(in_cache, suffix_scores, -jnp.inf)
        top_score = jnp.maximum(jnp.max(prefix_scores, axis=-1), jnp.max(suffix_scores, axis=-1))
        prefix_weights = jnp.exp(prefix_scores - top_score[..., None])
        suffix_weights = jnp.where(in_cache, jnp.exp(suffix_scores - top_score[..., None]), 0.0)
        weight_total = jnp.sum(prefix_weights, axis=-1) + jnp.sum(suffix_weights, axis=-1)
        rounded_prefix = lax.optimization_barrier(prefix_weights.astype(jnp.bfloat16)).astype(jnp.float32)
        rounded_suffix = lax.optimization_barrier(suffix_weights.astype(jnp.bfloat16)).astype(jnp.float32)
        summed = jnp.einsum("kgp,pkd->kgd", rounded_prefix, doc_values) + jnp.einsum("kgt,tkd->kgd", rounded_suffix, cache_values)
        return (summed / weight_total[..., None]).astype(jnp.bfloat16).reshape(H * HD)

    return lax.map(one_row, (queries, seq_doc[:, 0], suffix_lengths, suffix_keys, suffix_values))
```

```python
import jax
import jax.numpy as jnp
from jax import lax
from jax.experimental import pallas as pl
from jax.experimental.pallas import tpu as pltpu
from jax.sharding import PartitionSpec as P

H = 64
KVH = 8
HD = 128
G = H // KVH
SLOTS = 16
ROWS = 32
SLEN = 32
POS = 1024
HALF = KVH // 2
QCOLS = HALF * G * HD
NQ = 4 * G * SLOTS
NR = G * ROWS
STAT = 16
SCALE = 1.4426950408889634 / HD**0.5
MESH = pl.DeviceIdType.MESH
F32 = jnp.float32
BF16 = jnp.bfloat16


def dot(a, b, contract=((1,), (0,))):
    return lax.dot_general(a, b, (contract, ((), ())), preferred_element_type=F32)


def iota(shape, dim):
    return lax.broadcasted_iota(jnp.int32, shape, dim)


def in_three(value):
    high = value.astype(BF16).astype(F32)
    rest = value - high
    middle = rest.astype(BF16).astype(F32)
    return high, middle, rest - middle


def stat_rows(maxima, totals):
    width = maxima.shape[1]
    row = iota((STAT, width), 0)
    rows = jnp.zeros((STAT, width), F32)
    for place, value in enumerate(in_three(maxima) + in_three(totals)):
        rows = jnp.where(row == place, value, rows)
    return rows.astype(BF16)


def read_stats(rows):
    rows = rows.astype(F32)
    return rows[0:1] + rows[1:2] + rows[2:3], rows[3:4] + rows[4:5] + rows[5:6]


def merge(parts):
    top = parts[0][0]
    for part in parts[1:]:
        top = jnp.maximum(top, part[0])
    total, summed = 0.0, 0.0
    for maxima, totals, attended in parts:
        factor = jnp.exp2(maxima - top)
        total = total + totals * factor
        summed = summed + attended * factor
    return top, total, summed


def kernel(
    queries, docs, lengths, keys, values, suffix_keys, suffix_values, out,
    q_home, q_out, q_in, k_buf, v_buf, v_turned, sk_buf, sv_buf, s_out, s_stat,
    o_send, y_recv, x_send, h_recv, gathered,
    local_sem, kv_send, kv_recv, q_send, q_recv, y_ssem, y_rsem, x_ssem, x_rsem, g_ssem, g_rsem,
):
    ctx, batch = lax.axis_index("ctx"), lax.axis_index("batch")
    y, core = ctx // 2, ctx % 2
    x, z = batch // 4, batch % 4
    group = core * HALF + y

    def at_xz(dx, dz):
        return (ctx, ((x + dx) % 4) * 4 + (z + dz) % 4)

    def at_ctx(delta):
        return ((ctx + delta) % 8, batch)

    sibling = (y * 2 + (1 - core), batch)
    mine = pl.ds(pl.multiple_of(core * HALF * HD, HALF * HD), HALF * HD)
    theirs = pl.ds(pl.multiple_of((1 - core) * HALF * HD, HALF * HD), HALF * HD)
    group_cols = pl.ds(pl.multiple_of(group * HD, HD), HD)

    local = [
        pltpu.make_async_copy(
            queries.at[:, pl.ds(pl.multiple_of(core * QCOLS, QCOLS), QCOLS)], q_home, local_sem.at[0]
        ),
        pltpu.make_async_copy(keys.at[0, :, mine], k_buf.at[0], local_sem.at[1]),
        pltpu.make_async_copy(values.at[0, :, mine], v_buf.at[0], local_sem.at[2]),
        pltpu.make_async_copy(suffix_keys.at[:, :, group_cols], sk_buf, local_sem.at[3]),
        pltpu.make_async_copy(suffix_values.at[:, :, group_cols], sv_buf, local_sem.at[4]),
    ]
    for copy in local:
        copy.start()

    barrier = pltpu.get_barrier_semaphore()
    for dz in range(4):
        for dx in range(4):
            if dx or dz:
                pl.semaphore_signal(barrier, inc=1, device_id=at_xz(dx, dz), device_id_type=MESH)
    for delta in range(1, 8):
        pl.semaphore_signal(barrier, inc=1, device_id=at_ctx(delta), device_id_type=MESH)

    doc = jnp.bitwise_and(docs[...] - x + 4, 3)
    named = (iota((8, ROWS), 0) == doc).astype(F32)
    before = (iota((ROWS, ROWS), 0) < iota((ROWS, ROWS), 1)).astype(BF16)
    rank = jnp.sum(named * dot(named.astype(BF16), before), axis=0, keepdims=True)
    code = doc.astype(F32) * SLOTS + rank
    to_slots = (iota((4 * SLOTS, ROWS), 0).astype(F32) == code).astype(BF16)
    spread = (iota((ROWS, NR), 1) % ROWS == iota((ROWS, NR), 0)).astype(BF16)
    code_of = dot(jnp.broadcast_to(code, (8, ROWS)).astype(BF16), spread)[0:1]
    length_of = dot(jnp.broadcast_to(lengths[...], (8, ROWS)).astype(F32).astype(BF16), spread)[0:1]

    local[0].wait()
    for part in range(HALF):
        cols = slice(part * G * HD, (part + 1) * G * HD)
        slots = dot(to_slots, q_home[:, cols]).astype(BF16)
        for dx in range(4):
            q_out[dx, :, cols] = slots[dx * SLOTS : (dx + 1) * SLOTS]
    q_in[0, 0] = q_out[0]

    pl.semaphore_wait(barrier, 22)

    q_copies = {}
    for chunk in (0, 1, 2, 3):
        for place in range(4):
            if chunk or place:
                copy = pltpu.make_async_remote_copy(
                    src_ref=q_out.at[(4 - place) % 4],
                    dst_ref=q_in.at[chunk, place],
                    send_sem=q_send.at[chunk, place],
                    recv_sem=q_recv.at[chunk, place],
                    device_id=at_xz(4 - place, 4 - chunk),
                    device_id_type=MESH,
                )
                copy.start()
                q_copies[chunk, place] = copy
    kv_copies = [
        pltpu.make_async_remote_copy(
            src_ref=source.at[0, :, theirs],
            dst_ref=buffer.at[1],
            send_sem=kv_send.at[place],
            recv_sem=kv_recv.at[place],
            device_id=sibling,
            device_id_type=MESH,
        )
        for place, (source, buffer) in enumerate(((keys, k_buf), (values, v_buf)))
    ]
    for copy in kv_copies:
        copy.start()

    local[3].wait()
    local[4].wait()
    own = jnp.concatenate(
        [q_home[:, pl.ds(pl.multiple_of(y * G * HD + j * HD, HD), HD)] for j in range(G)], axis=0
    )
    scores = dot(sk_buf[...].reshape(ROWS * SLEN, HD), own, ((1,), (1,))) * SCALE
    row, col = iota((ROWS * SLEN, NR), 0), iota((ROWS * SLEN, NR), 1)
    live = (row // SLEN == col % ROWS) & ((row % SLEN).astype(F32) < length_of)
    scores = jnp.where(live, scores, -jnp.inf)
    top = jnp.max(scores, axis=0, keepdims=True)
    weights = jnp.where(live, jnp.exp2(scores - top), 0.0)
    s_stat[0:1] = top
    s_stat[1:2] = jnp.sum(weights, axis=0, keepdims=True)
    s_out[...] = dot(sv_buf[...].reshape(ROWS * SLEN, HD), weights.astype(BF16), ((0,), (0,)))

    def turn(source):
        def block(b, carry):
            rows = pl.ds(pl.multiple_of(b * 256, 256), 256)
            at = pl.ds(pl.multiple_of(source * POS + b * 256, 256), 256)
            v_turned[:, at] = jnp.transpose(v_buf[source, rows, :])
            return carry

        lax.fori_loop(0, POS // 256, block, 0)

    local[2].wait()
    turn(0)
    local[1].wait()
    kv_copies[0].wait_recv()
    kv_copies[1].wait_recv()
    turn(1)

    def attend(chunk):
        def head(h, carry):
            cols = pl.ds(pl.multiple_of(h * HD, HD), HD)
            q = jnp.concatenate(
                [
                    q_in[chunk, place, :, pl.ds(pl.multiple_of(h * G * HD + j * HD, HD), HD)]
                    for place in range(4)
                    for j in range(G)
                ],
                axis=0,
            )
            k = k_buf[:, :, cols].reshape(2 * POS, HD)
            scores = dot(k, q, ((1,), (1,)))
            top = jnp.max(scores, axis=0, keepdims=True) * SCALE
            weights = jnp.exp2(scores * SCALE - top)
            totals = jnp.sum(weights, axis=0, keepdims=True)
            attended = dot(v_turned[cols, :], weights.astype(BF16))
            o_send[chunk, h, 0:HD] = attended.astype(BF16)
            o_send[chunk, h, HD : HD + STAT] = stat_rows(top, totals)
            return carry

        lax.fori_loop(0, HALF, head, 0)

    y_copies, x_copies = {}, {}

    def send_y(chunk):
        for step in range(1, 4):
            copy = pltpu.make_async_remote_copy(
                src_ref=o_send.at[chunk, (y + step) % 4],
                dst_ref=y_recv.at[chunk, step - 1],
                send_sem=y_ssem.at[chunk, step - 1],
                recv_sem=y_rsem.at[chunk, step - 1],
                device_id=at_ctx(2 * step),
                device_id_type=MESH,
            )
            copy.start()
            y_copies[chunk, step] = copy

    def reduce_y(chunk):
        for step in range(1, 4):
            y_copies[chunk, step].wait_recv()

        def part(block):
            return read_stats(block[HD : HD + STAT]) + (block[0:HD].astype(F32),)

        parts = [part(o_send[chunk, y])] + [part(y_recv[chunk, i]) for i in range(3)]
        top, totals, attended = merge(parts)
        x_send[chunk, 0:HD] = attended.astype(BF16)
        x_send[chunk, HD : HD + STAT] = stat_rows(top, totals)
        for place in range(4):
            source = x_send.at[chunk, :, place * HD : (place + 1) * HD]
            back = (4 - place) % 4
            if chunk == 0 and place == 0:
                h_recv[0, :, 0:HD] = x_send[0, :, 0:HD]
                continue
            copy = pltpu.make_async_remote_copy(
                src_ref=source,
                dst_ref=h_recv.at[(4 - chunk) % 4, :, back * HD : (back + 1) * HD],
                send_sem=x_ssem.at[chunk, place],
                recv_sem=x_rsem.at[(4 - chunk) % 4, back],
                device_id=at_xz(place, chunk),
                device_id_type=MESH,
            )
            copy.start()
            x_copies[chunk, place] = copy

    for chunk in range(4):
        for place in range(4):
            if chunk or place:
                q_copies[chunk, place].wait_recv()
        attend(chunk)
        send_y(chunk)
        if chunk:
            reduce_y(chunk - 1)
    reduce_y(3)

    line = iota((NQ, NR), 0)
    place_of = (line // (G * SLOTS)) * SLOTS + line % SLOTS
    same_head = (line // SLOTS) % G == iota((NQ, NR), 1) // ROWS
    pick = (same_head & (place_of.astype(F32) == code_of)).astype(BF16)
    for copy in x_copies.values():
        copy.wait_recv()
    parts = [(s_stat[0:1], s_stat[1:2], s_out[...])]
    for source in range(4):
        rows = dot(h_recv[source], pick)
        parts.append(read_stats(rows[HD : HD + STAT]) + (rows[0:HD],))
    top, totals, attended = merge(parts)
    result = jnp.transpose(attended / totals).astype(BF16)
    block_cols = pl.ds(pl.multiple_of(group * G * HD, G * HD), G * HD)
    for j in range(G):
        gathered[:, pl.ds(pl.multiple_of(group * G * HD + j * HD, HD), HD)] = result[
            j * ROWS : (j + 1) * ROWS
        ]
    g_copies = []
    for delta in range(1, 8):
        copy = pltpu.make_async_remote_copy(
            src_ref=gathered.at[:, block_cols],
            dst_ref=gathered.at[:, block_cols],
            send_sem=g_ssem.at[delta - 1],
            recv_sem=g_rsem.at[delta - 1],
            device_id=at_ctx(delta),
            device_id_type=MESH,
        )
        copy.start()
        g_copies.append(copy)
    for delta in range(1, 8):
        source = (ctx + 8 - delta) % 8
        source_group = (source % 2) * HALF + source // 2
        source_cols = pl.ds(pl.multiple_of(source_group * G * HD, G * HD), G * HD)
        pltpu.make_async_remote_copy(
            src_ref=gathered.at[:, source_cols],
            dst_ref=gathered.at[:, source_cols],
            send_sem=g_ssem.at[delta - 1],
            recv_sem=g_rsem.at[delta - 1],
            device_id=at_ctx(delta),
            device_id_type=MESH,
        ).wait_recv()
    last = pltpu.make_async_copy(gathered, out, local_sem.at[5])
    last.start()
    for copies in (q_copies.values(), kv_copies, y_copies.values(), x_copies.values(), g_copies):
        for copy in copies:
            copy.wait_send()
    last.wait()


def on_device(queries, docs, lengths, keys, values, suffix_keys, suffix_values):
    anywhere = pl.BlockSpec(memory_space=pl.ANY)
    vmem = pl.BlockSpec(memory_space=pltpu.VMEM)
    dma = pltpu.SemaphoreType.DMA
    message = HD + STAT
    return pl.pallas_call(
        kernel,
        name="shared_prefix_attention",
        out_shape=jax.ShapeDtypeStruct((ROWS, H * HD), BF16),
        in_specs=[anywhere, vmem, vmem, anywhere, anywhere, anywhere, anywhere],
        out_specs=anywhere,
        scratch_shapes=[
            pltpu.VMEM((ROWS, QCOLS), BF16),
            pltpu.VMEM((4, SLOTS, QCOLS), BF16),
            pltpu.VMEM((4, 4, SLOTS, QCOLS), BF16),
            pltpu.VMEM((2, POS, HALF * HD), BF16),
            pltpu.VMEM((2, POS, HALF * HD), BF16),
            pltpu.VMEM((HALF * HD, 2 * POS), BF16),
            pltpu.VMEM((ROWS, SLEN, HD), BF16),
            pltpu.VMEM((ROWS, SLEN, HD), BF16),
            pltpu.VMEM((HD, NR), F32),
            pltpu.VMEM((8, NR), F32),
            pltpu.VMEM((4, HALF, message, NQ), BF16),
            pltpu.VMEM((4, 3, message, NQ), BF16),
            pltpu.VMEM((4, message, NQ), BF16),
            pltpu.VMEM((4, message, NQ), BF16),
            pltpu.VMEM((ROWS, H * HD), BF16),
            dma((6,)),
            dma((2,)),
            dma((2,)),
            dma((4, 4)),
            dma((4, 4)),
            dma((4, 3)),
            dma((4, 3)),
            dma((4, 4)),
            dma((4, 4)),
            dma((7,)),
            dma((7,)),
        ],
        compiler_params=pltpu.CompilerParams(
            collective_id=0, has_side_effects=True, vmem_limit_bytes=56 * 1024 * 1024
        ),
    )(
        queries, docs.reshape(1, ROWS), lengths.reshape(1, ROWS), keys, values, suffix_keys, suffix_values
    )


def solution(mesh):
    in_specs = (
        P("batch", None),
        P("batch", None),
        P("batch"),
        P("batch", "ctx", None),
        P("batch", "ctx", None),
        P("batch", None, None),
        P("batch", None, None),
    )
    return jax.shard_map(
        on_device, mesh=mesh, in_specs=in_specs, out_specs=P("batch", None), check_vma=False
    )
```

```python
import jax
import jax.numpy as jnp
from jax import lax
from jax.experimental import pallas as pl
from jax.experimental.pallas import tpu as pltpu
from jax.sharding import PartitionSpec as P

H = 64
KVH = 8
HD = 128
G = H // KVH
SLOTS = 16
ROWS = 32
SLEN = 32
POS = 1024
HALF = KVH // 2
QCOLS = HALF * G * HD
NQ = 4 * G * SLOTS
NR = G * ROWS
STAT = 16
BLOCK = 512
ORDER = (2, 1, 3, 0)
SCALE = 1.4426950408889634 / HD**0.5
MESH = pl.DeviceIdType.MESH
F32 = jnp.float32
BF16 = jnp.bfloat16


def dot(a, b, contract=((1,), (0,))):
    return lax.dot_general(a, b, (contract, ((), ())), preferred_element_type=F32)


def iota(shape, dim):
    return lax.broadcasted_iota(jnp.int32, shape, dim)


def in_three(value):
    high = value.astype(BF16).astype(F32)
    rest = value - high
    middle = rest.astype(BF16).astype(F32)
    return high, middle, rest - middle


def stat_rows(maxima, totals):
    width = maxima.shape[1]
    row = iota((STAT, width), 0)
    rows = jnp.zeros((STAT, width), F32)
    for place, value in enumerate(in_three(maxima) + in_three(totals)):
        rows = jnp.where(row == place, value, rows)
    return rows.astype(BF16)


def read_stats(rows):
    rows = rows.astype(F32)
    return rows[0:1] + rows[1:2] + rows[2:3], rows[3:4] + rows[4:5] + rows[5:6]


def merge(parts):
    top = parts[0][0]
    for part in parts[1:]:
        top = jnp.maximum(top, part[0])
    total, summed = 0.0, 0.0
    for maxima, totals, attended in parts:
        factor = jnp.exp2(maxima - top)
        total = total + totals * factor
        summed = summed + attended * factor
    return top, total, summed


def kernel(
    queries, docs, lengths, keys, values, suffix_keys, suffix_values, out,
    q_home, q_out, q_relay, q_in, k_buf, v_buf, v_turned, sk_buf, sv_buf, s_out, s_stat, pick,
    scores_a, scores_b, o_send, y_relay, y_merged, y_recv, x_send, h_recv, gathered,
    local_sem, out_sem, kv_ssem, kv_rsem, qx_ssem, qx_rsem, qz_ssem, qz_rsem, qzz_ssem, qzz_rsem,
    y_ssem, y_rsem, x_ssem, x_rsem, g_ssem, g_rsem,
):
    ctx, batch = lax.axis_index("ctx"), lax.axis_index("batch")
    y, core = ctx // 2, ctx % 2
    x, z = batch // 4, batch % 4
    group = core * HALF + y

    def at_xz(dx, dz):
        return (ctx, ((x + dx) % 4) * 4 + (z + dz) % 4)

    def at_y(dy):
        return ((ctx + 2 * dy) % 8, batch)

    sibling = (y * 2 + (1 - core), batch)

    def cols(start, width):
        return pl.ds(pl.multiple_of(start * width, width), width)

    def heads(i):
        return (y + ORDER[i]) % 4

    sent = []

    def send(src, dst, send_sem, recv_sem, device):
        copy = pltpu.make_async_remote_copy(
            src_ref=src,
            dst_ref=dst,
            send_sem=send_sem,
            recv_sem=recv_sem,
            device_id=device,
            device_id_type=MESH,
        )
        copy.start()
        sent.append(copy)
        return copy

    barrier = pltpu.get_barrier_semaphore()
    for dz in range(4):
        for dx in range(4):
            if dx or dz:
                pl.semaphore_signal(barrier, inc=1, device_id=at_xz(dx, dz), device_id_type=MESH)
    for dy in range(1, 4):
        pl.semaphore_signal(barrier, inc=1, device_id=at_y(dy), device_id_type=MESH)
    pl.semaphore_signal(barrier, inc=1, device_id=sibling, device_id_type=MESH)

    local = [
        pltpu.make_async_copy(queries.at[:, cols(core, QCOLS)], q_home, local_sem.at[0]),
        pltpu.make_async_copy(keys.at[0, :, cols(core, HALF * HD)], k_buf.at[0], local_sem.at[1]),
        pltpu.make_async_copy(values.at[0, :, cols(core, HALF * HD)], v_buf.at[0], local_sem.at[2]),
        pltpu.make_async_copy(suffix_keys.at[:, :, cols(group, HD)], sk_buf, local_sem.at[3]),
        pltpu.make_async_copy(suffix_values.at[:, :, cols(group, HD)], sv_buf, local_sem.at[4]),
    ]
    for copy in local:
        copy.start()

    doc = jnp.bitwise_and(docs[...] - x + 4, 3)
    named = (iota((8, ROWS), 0) == doc).astype(F32)
    before = (iota((ROWS, ROWS), 0) < iota((ROWS, ROWS), 1)).astype(BF16)
    rank = jnp.sum(named * dot(named.astype(BF16), before), axis=0, keepdims=True)
    code = doc.astype(F32) * SLOTS + rank
    to_slots = (iota((4 * SLOTS, ROWS), 0).astype(F32) == code).astype(BF16)

    local[0].wait()
    for i in range(HALF):
        slots = dot(to_slots, q_home[:, cols(heads(i), G * HD)]).astype(BF16)
        q_in[0, i, 0] = slots[0:SLOTS]
        for dx in range(1, 4):
            q_out[dx - 1, i] = slots[dx * SLOTS : (dx + 1) * SLOTS]

    pl.semaphore_wait(barrier, 19)

    sides = ((0, 1), (1, 3))
    half = (slice(0, 2), slice(2, 4))
    relay, direct, forwarded, first_hop, second_hop = {}, {}, {}, {}, {}
    for i in range(HALF):
        relay[i] = send(
            q_out.at[1, i], q_relay.at[i], qx_ssem.at[i, 2], qx_rsem.at[i, 2], at_xz((1, 3)[i % 2], 0)
        )
        for side, step in sides:
            direct[i, side] = send(
                q_out.at[step - 1, i],
                q_in.at[0, i, 4 - step],
                qx_ssem.at[i, side],
                qx_rsem.at[i, side],
                at_xz(step, 0),
            )

    def x_forward(i):
        relay[i].wait_recv()
        forwarded[i] = send(
            q_relay.at[i], q_in.at[0, i, 2], qx_ssem.at[i, 3], qx_rsem.at[i, 3], at_xz((1, 3)[i % 2], 0)
        )

    def z_first(i):
        direct[i, 0].wait_recv()
        direct[i, 1].wait_recv()
        forwarded[i].wait_recv()
        for side, step in sides:
            first_hop[i, side] = send(
                q_in.at[0, i],
                q_in.at[4 - step, i],
                qz_ssem.at[i, side],
                qz_rsem.at[i, side],
                at_xz(0, step),
            )

    def z_second(i):
        for side, step in sides:
            first_hop[i, side].wait_recv()
            second_hop[i, side] = send(
                q_in.at[4 - step, i, half[side]],
                q_in.at[2, i, half[side]],
                qzz_ssem.at[i, side],
                qzz_rsem.at[i, side],
                at_xz(0, step),
            )

    def z_last(i):
        second_hop[i, 0].wait_recv()
        second_hop[i, 1].wait_recv()

    kv_copies = [
        send(source.at[0, :, cols(1 - core, HALF * HD)], buffer.at[1], kv_ssem.at[i], kv_rsem.at[i], sibling)
        for i, (source, buffer) in enumerate(((keys, k_buf), (values, v_buf)))
    ]

    spread = (iota((ROWS, NR), 1) % ROWS == iota((ROWS, NR), 0)).astype(BF16)
    code_of = dot(jnp.broadcast_to(code, (8, ROWS)).astype(BF16), spread)[0:1]
    length_of = dot(jnp.broadcast_to(lengths[...], (8, ROWS)).astype(F32).astype(BF16), spread)[0:1]
    local[3].wait()
    local[4].wait()
    own = jnp.concatenate([q_home[:, cols(y * G + j, HD)] for j in range(G)], axis=0)
    scores = dot(sk_buf[...].reshape(ROWS * SLEN, HD), own, ((1,), (1,))) * SCALE
    row, col = iota((ROWS * SLEN, NR), 0), iota((ROWS * SLEN, NR), 1)
    live = (row // SLEN == col % ROWS) & ((row % SLEN).astype(F32) < length_of)
    scores = jnp.where(live, scores, -jnp.inf)
    top = jnp.max(scores, axis=0, keepdims=True)
    weights = jnp.where(live, jnp.exp2(scores - top), 0.0)
    s_stat[0:1] = top
    s_stat[1:2] = jnp.sum(weights, axis=0, keepdims=True)
    s_out[...] = dot(sv_buf[...].reshape(ROWS * SLEN, HD), weights.astype(BF16), ((0,), (0,)))

    def turn(source):
        def block(b, carry):
            rows = cols(b, 256)
            v_turned[:, cols(source * (POS // 256) + b, 256)] = jnp.transpose(v_buf[source, rows, :])
            return carry

        lax.fori_loop(0, POS // 256, block, 0)

    x_forward(0)
    x_forward(1)
    local[2].wait()
    turn(0)
    z_first(0)
    x_forward(2)
    x_forward(3)
    local[1].wait()
    for copy in kv_copies:
        copy.wait_recv()
    turn(1)

    line = iota((NQ, NR), 0)
    place_of = (line // (G * SLOTS)) * SLOTS + line % SLOTS
    same_head = (line // SLOTS) % G == iota((NQ, NR), 1) // ROWS
    pick[...] = (same_head & (place_of.astype(F32) == code_of)).astype(BF16)

    def score_block(chunk, i, q, b, target, top):
        at = (b * BLOCK) % POS
        k = k_buf[b * BLOCK // POS, at : at + BLOCK, cols(heads(i), HD)]
        scores = dot(k, q, ((1,), (1,)))
        target[b * BLOCK : (b + 1) * BLOCK] = scores
        here = jnp.max(scores.reshape(BLOCK // 8, 8, NQ), axis=0)
        return here if top is None else jnp.maximum(top, here)

    def value_block(i, b, source, top, state):
        weights = jnp.exp2(source[b * BLOCK : (b + 1) * BLOCK] * SCALE - top)
        totals = jnp.sum(weights.reshape(BLOCK // 8, 8, NQ), axis=0)
        attended = dot(
            v_turned[cols(heads(i), HD), b * BLOCK : (b + 1) * BLOCK], weights.astype(BF16)
        )
        return (totals, attended) if state is None else (state[0] + totals, state[1] + attended)

    def unit(now, top, source, then, target):
        state, later = None, None
        if then is not None:
            chunk, i = then
            q = jnp.concatenate(
                [q_in[chunk, i, place, :, j * HD : (j + 1) * HD] for place in range(4) for j in range(G)],
                axis=0,
            )
        for b in range(2 * POS // BLOCK):
            if then is not None:
                later = score_block(*then, q, b, target, later)
            if now is not None:
                state = value_block(now[1], b, source, top, state)
        if now is not None:
            o_send[now[0], now[1], 0:HD] = state[1].astype(BF16)
            o_send[now[0], now[1], HD : HD + STAT] = stat_rows(
                top, jnp.sum(state[0], axis=0, keepdims=True)
            )
        if then is not None:
            return jnp.max(later, axis=0, keepdims=True) * SCALE

    def part(block):
        return read_stats(block[HD : HD + STAT]) + (block[0:HD].astype(F32),)

    def packed(target, state):
        top, totals, attended = state
        target[0:HD] = attended.astype(BF16)
        target[HD : HD + STAT] = stat_rows(top, totals)

    lanes = (slice(0, NQ // 2), slice(NQ // 2, NQ))
    y_waits, x_waits = {}, {}

    def after(chunk, i):
        if i == 0:
            for side, step in ((0, 1), (1, 3)):
                y_waits[chunk, side] = send(
                    o_send.at[chunk, 0, :, lanes[side]],
                    y_relay.at[chunk, side],
                    y_ssem.at[chunk, side],
                    y_rsem.at[chunk, side],
                    at_y(step),
                )
        elif i < 3:
            side, step = i - 1, (1, 3)[i - 1]
            y_waits[chunk, 2 + side] = send(
                o_send.at[chunk, i, :, lanes[1 - side]],
                y_recv.at[chunk, side, 0],
                y_ssem.at[chunk, 2 + side],
                y_rsem.at[chunk, 2 + side],
                at_y(step),
            )
            y_waits[chunk, side].wait_recv()
            packed(
                y_merged.at[chunk, side],
                merge([part(o_send[chunk, i, :, lanes[side]]), part(y_relay[chunk, side])]),
            )
            y_waits[chunk, 4 + side] = send(
                y_merged.at[chunk, side],
                y_recv.at[chunk, side, 1],
                y_ssem.at[chunk, 4 + side],
                y_rsem.at[chunk, 4 + side],
                at_y(step),
            )

    def to_home(chunk):
        for i in range(2, 6):
            y_waits[chunk, i].wait_recv()
        for side in range(2):
            state = merge(
                [
                    part(o_send[chunk, 3, :, lanes[side]]),
                    part(y_recv[chunk, side, 1]),
                    part(y_recv[chunk, 1 - side, 0]),
                ]
            )
            packed(x_send.at[chunk, :, lanes[side]], state)
        for place in range(4):
            back = (4 - place) % 4
            source = x_send.at[chunk, :, place * HD : (place + 1) * HD]
            if chunk == 0 and place == 0:
                h_recv[0, :, 0:HD] = x_send[0, :, 0:HD]
                continue
            x_waits[(4 - chunk) % 4, back] = send(
                source,
                h_recv.at[(4 - chunk) % 4, :, back * HD : (back + 1) * HD],
                x_ssem.at[chunk, place],
                x_rsem.at[(4 - chunk) % 4, back],
                at_xz(place, chunk),
            )

    units = (
        (0, 0), (0, 1), (0, 2), (1, 0), (3, 0), (1, 1), (1, 2), (2, 0),
        (3, 1), (3, 2), (2, 1), (2, 2), (1, 3), (3, 3), (2, 3), (0, 3),
    )
    before_unit = {
        0: [(z_first, 1)],
        1: [(z_first, 2)],
        2: [(z_second, 0), (z_first, 3)],
        4: [(z_second, 1)],
        5: [(z_second, 2)],
        6: [(z_last, 0)],
        8: [(z_second, 3)],
        9: [(z_last, 1)],
        10: [(z_last, 2)],
        13: [(z_last, 3)],
    }
    buffers = (scores_a, scores_b)
    top = unit(None, None, None, units[0], buffers[0])
    for n, now in enumerate(units):
        then = units[n + 1] if n + 1 < len(units) else None
        for step, i in before_unit.get(n, ()):
            step(i)
        top = unit(now, top, buffers[n % 2], then, buffers[(n + 1) % 2])
        after(*now)
        if now[1] == 3:
            to_home(now[0])

    parts = [(s_stat[0:1], s_stat[1:2], s_out[...])]
    for source in (3, 1, 2, 0):
        for back in range(4):
            if source or back:
                x_waits[source, back].wait_recv()
        rows = dot(h_recv[source], pick[...])
        parts.append(read_stats(rows[HD : HD + STAT]) + (rows[0:HD],))
    top, totals, attended = merge(parts)
    result = jnp.transpose(attended / totals).astype(BF16)
    for j in range(G):
        gathered[:, cols(group * G + j, HD)] = result[j * ROWS : (j + 1) * ROWS]

    def block_of(dy, side):
        at = side * HALF + (y + dy) % 4
        return gathered.at[:, cols(at, G * HD)]

    written = []

    def write(dy, side):
        at = side * HALF + (y + dy) % 4
        copy = pltpu.make_async_copy(
            block_of(dy, side), out.at[:, cols(at, G * HD)], out_sem.at[0 if side is core else 1, dy]
        )
        copy.start()
        written.append(copy)

    def arrived(dy, side, place, device):
        pltpu.make_async_remote_copy(
            src_ref=block_of(dy, side),
            dst_ref=block_of(dy, side),
            send_sem=g_ssem.at[place],
            recv_sem=g_rsem.at[place],
            device_id=device,
            device_id_type=MESH,
        ).wait_recv()

    for dy in (2, 1, 3):
        send(block_of(0, core), block_of(0, core), g_ssem.at[dy], g_rsem.at[dy], at_y(dy))
    send(block_of(0, core), block_of(0, core), g_ssem.at[0], g_rsem.at[0], sibling)
    write(0, core)
    for dy in (1, 3, 2):
        back = 4 - dy
        arrived(back, core, dy, at_y(dy))
        send(block_of(back, core), block_of(back, core), g_ssem.at[3 + dy], g_rsem.at[3 + dy], sibling)
        write(back, core)
    for dy in (0, 1, 3, 2):
        arrived((4 - dy) % 4, 1 - core, 3 + dy if dy else 0, sibling)
        write((4 - dy) % 4, 1 - core)
    for copy in sent:
        copy.wait_send()
    for copy in written:
        copy.wait()


def on_device(queries, docs, lengths, keys, values, suffix_keys, suffix_values):
    anywhere = pl.BlockSpec(memory_space=pl.ANY)
    vmem = pl.BlockSpec(memory_space=pltpu.VMEM)
    dma = pltpu.SemaphoreType.DMA
    message = HD + STAT
    return pl.pallas_call(
        kernel,
        name="shared_prefix_attention",
        out_shape=jax.ShapeDtypeStruct((ROWS, H * HD), BF16),
        in_specs=[anywhere, vmem, vmem, anywhere, anywhere, anywhere, anywhere],
        out_specs=anywhere,
        scratch_shapes=[
            pltpu.VMEM((ROWS, QCOLS), BF16),
            pltpu.VMEM((3, HALF, SLOTS, G * HD), BF16),
            pltpu.VMEM((HALF, SLOTS, G * HD), BF16),
            pltpu.VMEM((4, 4, HALF, SLOTS, G * HD), BF16),
            pltpu.VMEM((2, POS, HALF * HD), BF16),
            pltpu.VMEM((2, POS, HALF * HD), BF16),
            pltpu.VMEM((HALF * HD, 2 * POS), BF16),
            pltpu.VMEM((ROWS, SLEN, HD), BF16),
            pltpu.VMEM((ROWS, SLEN, HD), BF16),
            pltpu.VMEM((HD, NR), F32),
            pltpu.VMEM((8, NR), F32),
            pltpu.VMEM((NQ, NR), BF16),
            pltpu.VMEM((2 * POS, NQ), F32),
            pltpu.VMEM((2 * POS, NQ), F32),
            pltpu.VMEM((4, HALF, message, NQ), BF16),
            pltpu.VMEM((4, 2, message, NQ // 2), BF16),
            pltpu.VMEM((4, 2, message, NQ // 2), BF16),
            pltpu.VMEM((4, 2, 2, message, NQ // 2), BF16),
            pltpu.VMEM((4, message, NQ), BF16),
            pltpu.VMEM((4, message, NQ), BF16),
            pltpu.VMEM((ROWS, H * HD), BF16),
            dma((5,)),
            dma((2, 4)),
            dma((2,)),
            dma((2,)),
            dma((4, 4)),
            dma((4, 4)),
            dma((4, 2)),
            dma((4, 2)),
            dma((4, 2)),
            dma((4, 2)),
            dma((4, 6)),
            dma((4, 6)),
            dma((4, 4)),
            dma((4, 4)),
            dma((7,)),
            dma((7,)),
        ],
        compiler_params=pltpu.CompilerParams(
            collective_id=0, has_side_effects=True, vmem_limit_bytes=56 * 1024 * 1024
        ),
    )(
        queries, docs.reshape(1, ROWS), lengths.reshape(1, ROWS), keys, values, suffix_keys, suffix_values
    )


def solution(mesh):
    in_specs = (
        P("batch", None),
        P("batch", None),
        P("batch"),
        P("batch", "ctx", None),
        P("batch", "ctx", None),
        P("batch", None, None),
        P("batch", None, None),
    )
    return jax.shard_map(
        on_device, mesh=mesh, in_specs=in_specs, out_specs=P("batch", None), check_vma=False
    )
```

```python
import jax
import jax.numpy as jnp
from jax import lax
from jax.experimental import pallas as pl
from jax.experimental.pallas import tpu as pltpu
from jax.sharding import PartitionSpec as P

H = 64
KVH = 8
HD = 128
G = H // KVH
SLOTS = 16
ROWS = 32
SLEN = 32
POS = 1024
HALF = KVH // 2
QCOLS = HALF * G * HD
NQ = 4 * G * SLOTS
NR = G * ROWS
STAT = 16
BLOCK = 512
ORDER = (2, 1, 3, 0)
SCALE = 1.4426950408889634 / HD**0.5
MESH = pl.DeviceIdType.MESH
F32 = jnp.float32
BF16 = jnp.bfloat16


def dot(a, b, contract=((1,), (0,))):
    return lax.dot_general(a, b, (contract, ((), ())), preferred_element_type=F32)


def iota(shape, dim):
    return lax.broadcasted_iota(jnp.int32, shape, dim)


def in_three(value):
    high = value.astype(BF16).astype(F32)
    rest = value - high
    middle = rest.astype(BF16).astype(F32)
    return high, middle, rest - middle


def stat_rows(maxima, totals):
    width = maxima.shape[1]
    row = iota((STAT, width), 0)
    rows = jnp.zeros((STAT, width), F32)
    for place, value in enumerate(in_three(maxima) + in_three(totals)):
        rows = jnp.where(row == place, value, rows)
    return rows.astype(BF16)


def read_stats(rows):
    rows = rows.astype(F32)
    return rows[0:1] + rows[1:2] + rows[2:3], rows[3:4] + rows[4:5] + rows[5:6]


def merge(parts):
    top = parts[0][0]
    for part in parts[1:]:
        top = jnp.maximum(top, part[0])
    total, summed = 0.0, 0.0
    for maxima, totals, attended in parts:
        factor = jnp.exp2(maxima - top)
        total = total + totals * factor
        summed = summed + attended * factor
    return top, total, summed


def kernel(
    queries, docs, lengths, keys, values, suffix_keys, suffix_values, out,
    q_home, q_out, q_relay, q_in, k_buf, v_buf, v_turned, sk_buf, sv_buf, s_out, s_stat, pick,
    scores_a, scores_b, o_send, y_relay, y_merged, y_recv, x_send, h_recv, gathered,
    local_sem, out_sem, kv_ssem, kv_rsem, qx_ssem, qx_rsem, qz_ssem, qz_rsem, qzz_ssem, qzz_rsem,
    y_ssem, y_rsem, x_ssem, x_rsem, g_ssem, g_rsem,
):
    ctx, batch = lax.axis_index("ctx"), lax.axis_index("batch")
    y, core = ctx // 2, ctx % 2
    x, z = batch // 4, batch % 4
    group = core * HALF + y

    def at_xz(dx, dz):
        return (ctx, ((x + dx) % 4) * 4 + (z + dz) % 4)

    def at_y(dy):
        return ((ctx + 2 * dy) % 8, batch)

    sibling = (y * 2 + (1 - core), batch)

    def cols(start, width):
        return pl.ds(pl.multiple_of(start * width, width), width)

    def heads(i):
        return (y + ORDER[i]) % 4

    sent = []

    def send(src, dst, send_sem, recv_sem, device):
        copy = pltpu.make_async_remote_copy(
            src_ref=src,
            dst_ref=dst,
            send_sem=send_sem,
            recv_sem=recv_sem,
            device_id=device,
            device_id_type=MESH,
        )
        copy.start()
        sent.append(copy)
        return copy

    barrier = pltpu.get_barrier_semaphore()
    for dz in range(4):
        for dx in range(4):
            if dx or dz:
                pl.semaphore_signal(barrier, inc=1, device_id=at_xz(dx, dz), device_id_type=MESH)
    for dy in range(1, 4):
        pl.semaphore_signal(barrier, inc=1, device_id=at_y(dy), device_id_type=MESH)
    pl.semaphore_signal(barrier, inc=1, device_id=sibling, device_id_type=MESH)

    local = [
        pltpu.make_async_copy(queries.at[:, cols(core, QCOLS)], q_home, local_sem.at[0]),
        pltpu.make_async_copy(keys.at[0, :, cols(core, HALF * HD)], k_buf.at[0], local_sem.at[1]),
        pltpu.make_async_copy(values.at[0, :, cols(core, HALF * HD)], v_buf.at[0], local_sem.at[2]),
        pltpu.make_async_copy(suffix_keys.at[:, :, cols(group, HD)], sk_buf, local_sem.at[3]),
        pltpu.make_async_copy(suffix_values.at[:, :, cols(group, HD)], sv_buf, local_sem.at[4]),
    ]
    for copy in local:
        copy.start()

    doc = jnp.bitwise_and(docs[...] - x + 4, 3)
    named = (iota((8, ROWS), 0) == doc).astype(F32)
    before = (iota((ROWS, ROWS), 0) < iota((ROWS, ROWS), 1)).astype(BF16)
    rank = jnp.sum(named * dot(named.astype(BF16), before), axis=0, keepdims=True)
    code = doc.astype(F32) * SLOTS + rank
    to_slots = (iota((4 * SLOTS, ROWS), 0).astype(F32) == code).astype(BF16)

    local[0].wait()
    for i in range(HALF):
        slots = dot(to_slots, q_home[:, cols(heads(i), G * HD)]).astype(BF16)
        q_in[0, i, 0] = slots[0:SLOTS]
        for dx in range(1, 4):
            q_out[dx - 1, i] = slots[dx * SLOTS : (dx + 1) * SLOTS]

    pl.semaphore_wait(barrier, 19)

    sides = ((0, 1), (1, 3))
    half = (slice(0, 2), slice(2, 4))
    relay, direct, forwarded, first_hop, second_hop = {}, {}, {}, {}, {}
    for i in range(HALF):
        relay[i] = send(
            q_out.at[1, i], q_relay.at[i], qx_ssem.at[i, 2], qx_rsem.at[i, 2], at_xz((1, 3)[i % 2], 0)
        )
        for side, step in sides:
            direct[i, side] = send(
                q_out.at[step - 1, i],
                q_in.at[0, i, 4 - step],
                qx_ssem.at[i, side],
                qx_rsem.at[i, side],
                at_xz(step, 0),
            )

    def x_forward(i):
        relay[i].wait_recv()
        forwarded[i] = send(
            q_relay.at[i], q_in.at[0, i, 2], qx_ssem.at[i, 3], qx_rsem.at[i, 3], at_xz((1, 3)[i % 2], 0)
        )

    def z_first(i):
        direct[i, 0].wait_recv()
        direct[i, 1].wait_recv()
        forwarded[i].wait_recv()
        for side, step in sides:
            first_hop[i, side] = send(
                q_in.at[0, i],
                q_in.at[4 - step, i],
                qz_ssem.at[i, side],
                qz_rsem.at[i, side],
                at_xz(0, step),
            )

    def z_second(i):
        for side, step in sides:
            first_hop[i, side].wait_recv()
            second_hop[i, side] = send(
                q_in.at[4 - step, i, half[side]],
                q_in.at[2, i, half[side]],
                qzz_ssem.at[i, side],
                qzz_rsem.at[i, side],
                at_xz(0, step),
            )

    def z_last(i):
        second_hop[i, 0].wait_recv()
        second_hop[i, 1].wait_recv()

    kv_copies = [
        send(source.at[0, :, cols(1 - core, HALF * HD)], buffer.at[1], kv_ssem.at[i], kv_rsem.at[i], sibling)
        for i, (source, buffer) in enumerate(((keys, k_buf), (values, v_buf)))
    ]

    spread = (iota((ROWS, NR), 1) % ROWS == iota((ROWS, NR), 0)).astype(BF16)
    code_of = dot(jnp.broadcast_to(code, (8, ROWS)).astype(BF16), spread)[0:1]
    length_of = dot(jnp.broadcast_to(lengths[...], (8, ROWS)).astype(F32).astype(BF16), spread)[0:1]
    def turn(source):
        def block(b, carry):
            rows = cols(b, 256)
            v_turned[:, cols(source * (POS // 256) + b, 256)] = jnp.transpose(v_buf[source, rows, :])
            return carry

        lax.fori_loop(0, POS // 256, block, 0)

    x_forward(0)
    x_forward(1)
    local[2].wait()
    turn(0)
    z_first(0)
    x_forward(2)
    x_forward(3)
    local[1].wait()
    for copy in kv_copies:
        copy.wait_recv()
    turn(1)

    line = iota((NQ, NR), 0)
    place_of = (line // (G * SLOTS)) * SLOTS + line % SLOTS
    same_head = (line // SLOTS) % G == iota((NQ, NR), 1) // ROWS
    pick[...] = (same_head & (place_of.astype(F32) == code_of)).astype(BF16)

    def score_block(chunk, i, q, b, target, top):
        at = (b * BLOCK) % POS
        k = k_buf[b * BLOCK // POS, at : at + BLOCK, cols(heads(i), HD)]
        scores = dot(k, q, ((1,), (1,)))
        target[b * BLOCK : (b + 1) * BLOCK] = scores
        here = jnp.max(scores.reshape(BLOCK // 8, 8, NQ), axis=0)
        return here if top is None else jnp.maximum(top, here)

    def value_block(i, b, source, top, state):
        weights = jnp.exp2(source[b * BLOCK : (b + 1) * BLOCK] * SCALE - top)
        totals = jnp.sum(weights.reshape(BLOCK // 8, 8, NQ), axis=0)
        attended = dot(
            v_turned[cols(heads(i), HD), b * BLOCK : (b + 1) * BLOCK], weights.astype(BF16)
        )
        return (totals, attended) if state is None else (state[0] + totals, state[1] + attended)

    lanes = (slice(0, NQ // 2), slice(NQ // 2, NQ))

    def unit(now, top, source, then, target):
        state, later = None, None
        if then is not None:
            chunk, i = then
            q = jnp.concatenate(
                [q_in[chunk, i, place, :, j * HD : (j + 1) * HD] for place in range(4) for j in range(G)],
                axis=0,
            )
        for b in range(2 * POS // BLOCK):
            if then is not None:
                later = score_block(*then, q, b, target, later)
            if now is not None:
                state = value_block(now[1], b, source, top, state)
        if now is not None:
            attended = state[1].astype(BF16)
            stats = stat_rows(top, jnp.sum(state[0], axis=0, keepdims=True))
            for side in range(2):
                o_send[now[0], now[1], side, 0:HD] = attended[:, lanes[side]]
                o_send[now[0], now[1], side, HD : HD + STAT] = stats[:, lanes[side]]
        if then is not None:
            return jnp.max(later, axis=0, keepdims=True) * SCALE

    def part(block):
        return read_stats(block[HD : HD + STAT]) + (block[0:HD].astype(F32),)

    def packed(target, state):
        top, totals, attended = state
        target[0:HD] = attended.astype(BF16)
        target[HD : HD + STAT] = stat_rows(top, totals)

    y_waits, x_waits = {}, {}

    def after(chunk, i):
        if i == 0:
            for side, step in ((0, 1), (1, 3)):
                y_waits[chunk, side] = send(
                    o_send.at[chunk, 0, side],
                    y_relay.at[chunk, side],
                    y_ssem.at[chunk, side],
                    y_rsem.at[chunk, side],
                    at_y(step),
                )
        elif i < 3:
            side, step = i - 1, (1, 3)[i - 1]
            y_waits[chunk, 2 + side] = send(
                o_send.at[chunk, i, 1 - side],
                y_recv.at[chunk, side, 0],
                y_ssem.at[chunk, 2 + side],
                y_rsem.at[chunk, 2 + side],
                at_y(step),
            )
            y_waits[chunk, side].wait_recv()
            packed(
                y_merged.at[chunk, side],
                merge([part(o_send[chunk, i, side]), part(y_relay[chunk, side])]),
            )
            y_waits[chunk, 4 + side] = send(
                y_merged.at[chunk, side],
                y_recv.at[chunk, side, 1],
                y_ssem.at[chunk, 4 + side],
                y_rsem.at[chunk, 4 + side],
                at_y(step),
            )

    def to_home(chunk):
        for i in range(2, 6):
            y_waits[chunk, i].wait_recv()
        for side in range(2):
            state = merge(
                [
                    part(o_send[chunk, 3, side]),
                    part(y_recv[chunk, side, 1]),
                    part(y_recv[chunk, 1 - side, 0]),
                ]
            )
            attended, stats = state[2].astype(BF16), stat_rows(state[0], state[1])
            for place in range(2):
                x_send[chunk, 2 * side + place, 0:HD] = attended[:, place * HD : (place + 1) * HD]
                x_send[chunk, 2 * side + place, HD : HD + STAT] = stats[:, place * HD : (place + 1) * HD]
        for place in range(4):
            back = (4 - place) % 4
            source = x_send.at[chunk, place]
            if chunk == 0 and place == 0:
                h_recv[0, 0] = x_send[0, 0]
                continue
            x_waits[(4 - chunk) % 4, back] = send(
                source,
                h_recv.at[(4 - chunk) % 4, back],
                x_ssem.at[chunk, place],
                x_rsem.at[(4 - chunk) % 4, back],
                at_xz(place, chunk),
            )

    units = (
        (0, 0), (0, 1), (0, 2), (1, 0), (3, 0), (1, 1), (1, 2), (2, 0),
        (3, 1), (3, 2), (2, 1), (2, 2), (1, 3), (3, 3), (2, 3), (0, 3),
    )
    before_unit = {
        0: [(z_first, 1)],
        1: [(z_first, 2)],
        2: [(z_second, 0), (z_first, 3)],
        4: [(z_second, 1)],
        5: [(z_second, 2)],
        6: [(z_last, 0)],
        8: [(z_second, 3)],
        9: [(z_last, 1)],
        10: [(z_last, 2)],
        13: [(z_last, 3)],
    }
    buffers = (scores_a, scores_b)
    top = unit(None, None, None, units[0], buffers[0])
    for n, now in enumerate(units):
        then = units[n + 1] if n + 1 < len(units) else None
        for step, i in before_unit.get(n, ()):
            step(i)
        top = unit(now, top, buffers[n % 2], then, buffers[(n + 1) % 2])
        after(*now)
        if now[1] == 3:
            to_home(now[0])

    local[3].wait()
    local[4].wait()
    own = jnp.concatenate([q_home[:, cols(y * G + j, HD)] for j in range(G)], axis=0)
    scores = dot(sk_buf[...].reshape(ROWS * SLEN, HD), own, ((1,), (1,))) * SCALE
    row, col = iota((ROWS * SLEN, NR), 0), iota((ROWS * SLEN, NR), 1)
    live = (row // SLEN == col % ROWS) & ((row % SLEN).astype(F32) < length_of)
    scores = jnp.where(live, scores, -jnp.inf)
    top = jnp.max(scores, axis=0, keepdims=True)
    weights = jnp.where(live, jnp.exp2(scores - top), 0.0)
    s_stat[0:1] = top
    s_stat[1:2] = jnp.sum(weights, axis=0, keepdims=True)
    s_out[...] = dot(sv_buf[...].reshape(ROWS * SLEN, HD), weights.astype(BF16), ((0,), (0,)))

    parts = [(s_stat[0:1], s_stat[1:2], s_out[...])]
    for source in (3, 1, 2, 0):
        for back in range(4):
            if source or back:
                x_waits[source, back].wait_recv()
        rows = dot(jnp.concatenate([h_recv[source, back] for back in range(4)], axis=1), pick[...])
        parts.append(read_stats(rows[HD : HD + STAT]) + (rows[0:HD],))
    top, totals, attended = merge(parts)
    result = jnp.transpose(attended / totals).astype(BF16)
    for j in range(G):
        gathered[:, cols(group * G + j, HD)] = result[j * ROWS : (j + 1) * ROWS]

    def block_of(dy, side):
        at = side * HALF + (y + dy) % 4
        return gathered.at[:, cols(at, G * HD)]

    written = []

    def write(dy, side):
        at = side * HALF + (y + dy) % 4
        copy = pltpu.make_async_copy(
            block_of(dy, side), out.at[:, cols(at, G * HD)], out_sem.at[0 if side is core else 1, dy]
        )
        copy.start()
        written.append(copy)

    def arrived(dy, side, place, device):
        pltpu.make_async_remote_copy(
            src_ref=block_of(dy, side),
            dst_ref=block_of(dy, side),
            send_sem=g_ssem.at[place],
            recv_sem=g_rsem.at[place],
            device_id=device,
            device_id_type=MESH,
        ).wait_recv()

    for dy in (2, 1, 3):
        send(block_of(0, core), block_of(0, core), g_ssem.at[dy], g_rsem.at[dy], at_y(dy))
    send(block_of(0, core), block_of(0, core), g_ssem.at[0], g_rsem.at[0], sibling)
    write(0, core)
    for dy in (1, 3, 2):
        back = 4 - dy
        arrived(back, core, dy, at_y(dy))
        send(block_of(back, core), block_of(back, core), g_ssem.at[3 + dy], g_rsem.at[3 + dy], sibling)
        write(back, core)
    for dy in (0, 1, 3, 2):
        arrived((4 - dy) % 4, 1 - core, 3 + dy if dy else 0, sibling)
        write((4 - dy) % 4, 1 - core)
    for copy in sent:
        copy.wait_send()
    for copy in written:
        copy.wait()


def on_device(queries, docs, lengths, keys, values, suffix_keys, suffix_values):
    anywhere = pl.BlockSpec(memory_space=pl.ANY)
    vmem = pl.BlockSpec(memory_space=pltpu.VMEM)
    dma = pltpu.SemaphoreType.DMA
    message = HD + STAT
    return pl.pallas_call(
        kernel,
        name="shared_prefix_attention",
        out_shape=jax.ShapeDtypeStruct((ROWS, H * HD), BF16),
        in_specs=[anywhere, vmem, vmem, anywhere, anywhere, anywhere, anywhere],
        out_specs=anywhere,
        scratch_shapes=[
            pltpu.VMEM((ROWS, QCOLS), BF16),
            pltpu.VMEM((3, HALF, SLOTS, G * HD), BF16),
            pltpu.VMEM((HALF, SLOTS, G * HD), BF16),
            pltpu.VMEM((4, 4, HALF, SLOTS, G * HD), BF16),
            pltpu.VMEM((2, POS, HALF * HD), BF16),
            pltpu.VMEM((2, POS, HALF * HD), BF16),
            pltpu.VMEM((HALF * HD, 2 * POS), BF16),
            pltpu.VMEM((ROWS, SLEN, HD), BF16),
            pltpu.VMEM((ROWS, SLEN, HD), BF16),
            pltpu.VMEM((HD, NR), F32),
            pltpu.VMEM((8, NR), F32),
            pltpu.VMEM((NQ, NR), BF16),
            pltpu.VMEM((2 * POS, NQ), F32),
            pltpu.VMEM((2 * POS, NQ), F32),
            pltpu.VMEM((4, HALF, 2, message, NQ // 2), BF16),
            pltpu.VMEM((4, 2, message, NQ // 2), BF16),
            pltpu.VMEM((4, 2, message, NQ // 2), BF16),
            pltpu.VMEM((4, 2, 2, message, NQ // 2), BF16),
            pltpu.VMEM((4, 4, message, HD), BF16),
            pltpu.VMEM((4, 4, message, HD), BF16),
            pltpu.VMEM((ROWS, H * HD), BF16),
            dma((5,)),
            dma((2, 4)),
            dma((2,)),
            dma((2,)),
            dma((4, 4)),
            dma((4, 4)),
            dma((4, 2)),
            dma((4, 2)),
            dma((4, 2)),
            dma((4, 2)),
            dma((4, 6)),
            dma((4, 6)),
            dma((4, 4)),
            dma((4, 4)),
            dma((7,)),
            dma((7,)),
        ],
        compiler_params=pltpu.CompilerParams(
            collective_id=0, has_side_effects=True, vmem_limit_bytes=56 * 1024 * 1024
        ),
    )(
        queries, docs.reshape(1, ROWS), lengths.reshape(1, ROWS), keys, values, suffix_keys, suffix_values
    )


def solution(mesh):
    in_specs = (
        P("batch", None),
        P("batch", None),
        P("batch"),
        P("batch", "ctx", None),
        P("batch", "ctx", None),
        P("batch", None, None),
        P("batch", None, None),
    )
    return jax.shard_map(
        on_device, mesh=mesh, in_specs=in_specs, out_specs=P("batch", None), check_vma=False
    )
```
